1024 devices in a mesh: dp: 4 (over y_hi), edata: 4 (over x), expert: 64 (over z, y_lo, core).
Axes of the slice: x: 4, y: 8 (y_hi: 4, y_lo: 2; y = y_hi * 2 + y_lo), z: 16, core: 2. Of those that a mesh axis runs over, the one named last changes fastest.
Arguments:
- out_grad: bfloat16 [131072, 3584], P(('dp', 'edata', 'expert')), may hold values from -4 to 4
- route_ids: int32 [131072, 8], P(('dp', 'edata', 'expert')), may hold values from 0 to 255, as said below
- router_logits: float32 [131072, 8], P(('dp', 'edata', 'expert')), may hold values from -8 to 8
- hidden: bfloat16 [16, 64, 192, 1024], P(('dp', 'edata'), 'expert'), may hold values from -6 to 6
- down_weight: bfloat16 [3584, 64, 1024], P(None, 'expert'), may hold values from -0.375 to 0.375
Outputs:
- grad_down: bfloat16 [3584, 64, 1024], P(('dp', 'edata'), 'expert')
- grad_hidden: bfloat16 [16, 64, 192, 1024], P(('dp', 'edata'), 'expert')
- logit_grad: float32 [131072, 8], P(('dp', 'edata', 'expert'))
The draws below stay inside these ranges and needn't reach their ends.
Inputs may be any that keep to these rules, and one draw needn't show every extreme that they name: `route_ids`: each row names 8 different experts. Within the rows of one device no expert below 64 is named more than 3 times, and on every device one of them is named exactly 3 times.
All inputs are finite; a program needn't handle non-finite values.
Results may differ from the reference program's by a relative error of at most 0.019.
Values may be sent and summed in bfloat16 or wider, within the bound.
A program may use at most 64 MiB of HBM per device.

```python
import jax
import jax.numpy as jnp
from jax import lax

D = 3584
H = 1024
TOP = 8
ROUTED = 256
EXPERTS = 64
CAP = 3
TOK_DEV = 128
GROUPS = 16
SLOTS = 192
TOKENS = 131072
N_DP = 4
N_EDATA = 4
N_EXPERT = 64


def draw_route_ids(key, part):
    key = jax.random.fold_in(key, 11)
    keys = jax.random.split(key, 5)
    blocks = TOKENS // TOK_DEV
    entries = TOK_DEV * TOP
    others = ROUTED - EXPERTS
    window = jax.random.randint(keys[0], (blocks, EXPERTS), 0, CAP + 1).astype(jnp.int32)
    peak = jax.random.randint(keys[1], (blocks,), 0, EXPERTS).astype(jnp.int32)
    window = jnp.where(jnp.arange(EXPERTS, dtype=jnp.int32)[None, :] == peak[:, None], CAP, window).astype(jnp.int32)
    remain = entries - jnp.sum(window, axis=1)
    base_count = remain // others
    extra_count = remain % others
    order = jax.random.permutation(keys[2], others).astype(jnp.int32)
    outside = base_count[:, None] + (order[None, :] < extra_count[:, None]).astype(jnp.int32)
    counts = jnp.concatenate([window, outside], axis=1)
    ends = jnp.cumsum(counts, axis=1)
    places = jnp.arange(entries, dtype=jnp.int32)
    expert_at = jax.vmap(lambda edges: jnp.searchsorted(edges, places, side='right'))(ends).astype(jnp.int32)
    table = jnp.transpose(expert_at.reshape(blocks, TOP, TOK_DEV), (0, 2, 1))
    token_keys = jax.random.split(keys[3], blocks)
    token_order = jax.vmap(lambda k: jax.random.permutation(k, TOK_DEV))(token_keys)
    table = jnp.take_along_axis(table, token_order[:, :, None], axis=1)
    table = table.reshape(blocks * TOK_DEV, TOP)
    column_keys = jax.random.split(keys[4], blocks * TOK_DEV)
    column_order = jax.vmap(lambda k: jax.random.permutation(k, TOP))(column_keys)
    table = jnp.take_along_axis(table, column_order, axis=1)
    return table.astype(jnp.int32)


def level_of(stream_key, shape, cuts, least, largest):
    factor_of = 1.0
    for axis_at, parts in cuts:
        steps = jax.random.uniform(jax.random.fold_in(jax.random.fold_in(stream_key, 6), axis_at), (parts,), jnp.float32, least / len(cuts), largest / len(cuts))
        factor_of = factor_of * jnp.repeat(jnp.exp(steps), shape[axis_at] // parts).reshape((-1,) + (1,) * (len(shape) - 1 - axis_at))
    return factor_of


def scatter_about(key, extent, deviation, bound, cuts=(), kind=jnp.bfloat16):
    loudness = level_of(key, extent, cuts, -0.22, 0.18) if cuts else 1.0
    values = jax.random.normal(key, extent, jnp.float32) * deviation * loudness
    return jnp.minimum(jnp.maximum(values, -bound), bound).astype(kind)


def setup_inputs(seed: int = 0) -> dict:
    splits = jax.random.split(jax.random.key(seed), 6)
    return {
        "out_grad": scatter_about(splits[0], (TOKENS, D), 0.3, 4.0, ((0, 1024),)),
        "route_ids": draw_route_ids(jax.random.fold_in(splits[5], 71), 0),
        "router_logits": scatter_about(splits[2], (TOKENS, TOP), 2.0, 8.0, ((0, 1024),), jnp.float32),
        "hidden": scatter_about(splits[3], (GROUPS, EXPERTS, SLOTS, H), 1.0, 6.0, ((0, 16), (1, 64))),
        "down_weight": scatter_about(splits[4], (D, EXPERTS, H), (H // 4) ** -0.5, 0.375, ((1, 64),)),
    }


def reference(out_grad, route_ids, router_logits, hidden, down_weight):
    groups = N_DP * N_EDATA
    slot_total = N_EXPERT * CAP
    device_blocks = TOKENS // TOK_DEV
    scores = jax.nn.sigmoid(router_logits)
    score_sum = jnp.sum(scores, axis=1, keepdims=True)
    combine = 2.5 * scores / score_sum
    combine_send = lax.optimization_barrier(combine.astype(jnp.bfloat16)).astype(jnp.float32)
    flat_routes = route_ids.reshape(device_blocks, TOK_DEV * TOP)
    onehot = (flat_routes[:, :, None] == jnp.arange(EXPERTS, dtype=jnp.int32)[None, None, :]).astype(jnp.int32)
    rank_in_device = jnp.sum((jnp.cumsum(onehot, axis=1) - 1) * onehot, axis=2).reshape(TOKENS, TOP).astype(jnp.int32)
    block_index = jnp.arange(TOKENS, dtype=jnp.int32) // TOK_DEV
    slot_base = (block_index // N_EXPERT) * slot_total + (block_index % N_EXPERT) * CAP
    filled = groups * slot_total

    def per_expert(running, inputs):
        expert, weight_e, hidden_e = inputs
        names_expert = route_ids == expert
        present = jnp.any(names_expert, axis=1)
        rank_e = jnp.sum(jnp.where(names_expert, rank_in_device, 0), axis=1).astype(jnp.int32)
        target = jnp.where(present, slot_base + rank_e, filled).astype(jnp.int32)
        slot_rows = jnp.zeros((filled, D), jnp.bfloat16).at[target].set(out_grad, mode="drop")
        chosen_weight = jnp.sum(jnp.where(names_expert, combine_send, 0.0), axis=1)
        weight = jnp.zeros((filled,), jnp.float32).at[target].set(chosen_weight, mode="drop")
        hidden_rows = hidden_e.reshape(filled, H)
        projected = jnp.dot(slot_rows, weight_e, preferred_element_type=jnp.float32)
        grad_hidden_e = (weight[:, None] * projected).astype(jnp.bfloat16)
        scaled = (weight[:, None] * slot_rows.astype(jnp.float32)).astype(jnp.bfloat16)
        slot_grad = jnp.sum(hidden_rows.astype(jnp.float32) * projected, axis=1)

        def add_group(accumulated, group_pair):
            partial_value = jnp.dot(group_pair[0].T, group_pair[1], preferred_element_type=jnp.float32)
            return accumulated + lax.optimization_barrier(partial_value.astype(jnp.bfloat16)).astype(jnp.float32), None

        accumulated, _ = lax.scan(add_group, jnp.zeros((D, H), jnp.float32), (scaled.reshape(groups, slot_total, D), hidden_e))
        safe_target = jnp.clip(target, 0, filled - 1).astype(jnp.int32)
        gathered = jnp.where(present, slot_grad[safe_target], 0.0)
        running = running + jnp.where(names_expert, gathered[:, None], 0.0)
        return running, (accumulated.astype(jnp.bfloat16), grad_hidden_e.reshape(groups, slot_total, H))

    inputs = (jnp.arange(EXPERTS, dtype=jnp.int32), jnp.moveaxis(down_weight, 1, 0), jnp.moveaxis(hidden, 1, 0))
    combine_grad, (down_parts, hidden_parts) = lax.scan(per_expert, jnp.zeros((TOKENS, TOP), jnp.float32), inputs)
    grad_down = jnp.moveaxis(down_parts, 0, 1)
    grad_hidden = jnp.moveaxis(hidden_parts, 0, 1)
    weighted_mean = jnp.sum(combine_grad * scores, axis=1, keepdims=True) / score_sum
    logit_grad = scores * (1.0 - scores) * (2.5 / score_sum) * (combine_grad - weighted_mean)
    return grad_down, grad_hidden, logit_grad
```

```python
import jax
import jax.numpy as jnp
from jax import lax
from jax.experimental import pallas as pl
from jax.experimental.pallas import tpu as pltpu
from jax.sharding import PartitionSpec as P

MESH = pl.DeviceIdType.MESH
BF = jnp.bfloat16
F32 = jnp.float32
NZ = 16
NJ = 4
NX = 4
NY = 4
CAP = 3
TOK = 128
TOP = 8
D = 3584
H = 1024
SLOTS = NZ * NJ * CAP
PLANE_ROWS = NZ * CAP
ZROWS = 16
CH = 512
NCH = D // CH
FOLD = CH // 128 - 1
BLK = D // NY
OWN = BLK // NX
PAD = 256
LAG = 3
OFFS = [8, 7, 9, 6, 10, 5, 11, 4, 12, 3, 13, 2, 14, 1, 15]


def iota(shape, axis):
    return lax.broadcasted_iota(jnp.int32, shape, axis)


def dot(a, b):
    return jnp.dot(a, b, preferred_element_type=F32)


def exact_dot(a, b):
    return jnp.dot(a, b, preferred_element_type=F32, precision=lax.Precision.HIGHEST)


def slot_parts(row):
    j = (row * 1366) >> 16
    rest = row - 48 * j
    z = (rest * 43) >> 7
    return j, z, rest - 3 * z


def fold_slot(row, part):
    z = row >> 4
    q = row & 15
    if part == 0:
        valid, s = q < 12, q
    else:
        valid, s = q >= 12, 4 * (part - 1) + (q - 12)
    j = (s * 11) >> 5
    return jnp.where(valid, z * NJ + j, -1), s - 3 * j


def named(ids, weights, expert):
    rows = expert.shape[0]
    count = jnp.zeros((rows, TOK), F32)
    weight = jnp.zeros((rows, TOK), F32)
    for k in range(TOP):
        hit = ids[k : k + 1, :] == expert
        count = count + jnp.where(hit, 1.0, 0.0)
        weight = weight + jnp.where(hit, weights[k : k + 1, :], 0.0)
    before = (iota((TOK, TOK), 0) < iota((TOK, TOK), 1)).astype(F32).astype(BF)
    rank = dot(count.astype(BF), before)
    return count, weight, rank


def kernel(
    og_hbm, ids_hbm, logit_hbm, hid_hbm, w_hbm,
    gd_hbm, gh_hbm, lg_hbm,
    og_s, ids_s, logit_s, hid_s, w_s, sel_s, unf_s, h4, zs, zr, ps, ar, xs, xr, ys, yr, proj,
    cnt_s, rank_s, r1s, r1r, r2s, r2r, gd_s, gh_s, lg_s,
    in_sem, out_sem, hs_sem, hr_sem, zs_sem, zr_sem, zl_sem, ps_sem, pr_sem, pl_sem,
    xs_sem, xr_sem, xl_sem, ys_sem, yr_sem, r_sem,
):
    dp = lax.axis_index("dp")
    ed = lax.axis_index("edata")
    ex = lax.axis_index("expert")
    z = ex // NJ
    j = ex % NJ
    core = ex % 2

    def at_z(h):
        return lax.rem(z + h, NZ)

    def at_j(h):
        return lax.rem(j + h, NJ)

    def at_x(h):
        return lax.rem(ed + h, NX)

    def to_z(zt):
        return {"expert": zt * NJ + j}

    def to_j(jt):
        return {"expert": z * NJ + jt}

    def owner(b, c):
        step = (2, 1, 3, 0)[b] if not isinstance(c, int) else ((2, 1, 3, 0), (2, 3, 1, 0))[c][b]
        if not isinstance(c, int) and b in (1, 2):
            step = jnp.where(c == 0, step, 4 - step)
        return lax.rem(dp + step, NY)

    def remote(src, dst, ssem, rsem, where):
        return pltpu.make_async_remote_copy(
            src_ref=src, dst_ref=dst, send_sem=ssem, recv_sem=rsem, device_id=where, device_id_type=MESH
        )

    barrier = pltpu.get_barrier_semaphore()
    for h in OFFS:
        pl.semaphore_signal(barrier, inc=1, device_id=to_z(at_z(h)), device_id_type=MESH)
    for h in range(1, 4):
        pl.semaphore_signal(barrier, inc=1, device_id=to_j(at_j(h)), device_id_type=MESH)
        pl.semaphore_signal(barrier, inc=1, device_id={"edata": at_x(h)}, device_id_type=MESH)
        pl.semaphore_signal(barrier, inc=1, device_id={"dp": lax.rem(dp + h, NY)}, device_id_type=MESH)

    pltpu.make_async_copy(ids_hbm, ids_s, in_sem.at[0]).start()
    pltpu.make_async_copy(logit_hbm, logit_s, in_sem.at[1]).start()
    for c in range(2):
        for b in range(NY):
            start = pl.multiple_of(owner(b, c) * BLK, BLK)
            pltpu.make_async_copy(
                og_hbm.at[:, pl.ds(start, BLK)],
                og_s.at[pl.ds(c * TOK, TOK), pl.ds(b * BLK, BLK)],
                in_sem.at[2],
            ).start()
    pltpu.make_async_copy(hid_hbm, hid_s, in_sem.at[3]).start()
    for b in range(NY):
        start = pl.multiple_of(owner(b, core) * BLK, BLK)
        pltpu.make_async_copy(
            w_hbm.at[pl.ds(start, BLK)], w_s.at[pl.ds(b * BLK, BLK)], in_sem.at[4]
        ).start()

    pltpu.make_async_copy(ids_hbm, ids_s, in_sem.at[0]).wait()
    pltpu.make_async_copy(logit_hbm, logit_s, in_sem.at[1]).wait()
    ids = ids_s[...]
    scores = jax.nn.sigmoid(logit_s[...])
    score_sum = jnp.sum(scores, axis=0, keepdims=True)
    weights = (2.5 * scores / score_sum).astype(BF).astype(F32)
    rows = NZ * ZROWS
    for part in range(1 + FOLD):
        expert, rank_of = fold_slot(iota((rows, 1), 0), part)
        count, weight, rank = named(ids, weights, expert)
        chosen = jnp.where((count > 0.0) & (rank == rank_of.astype(F32)), weight, 0.0)
        odd = (expert & 1) == 1
        sel_s[pl.ds(part * rows, rows), pl.ds(0, TOK)] = jnp.where(odd, 0.0, chosen).astype(BF)
        sel_s[pl.ds(part * rows, rows), pl.ds(TOK, TOK)] = jnp.where(odd, chosen, 0.0).astype(BF)
    count, _, rank = named(ids, weights, iota((NZ * NJ, 1), 0))
    cnt_s[...] = count
    rank_s[...] = rank

    jr, zrow, rk = slot_parts(iota((SLOTS, 1), 0))
    col = iota((SLOTS, rows), 1)
    same = (col >> 4) == zrow
    s = 3 * jr + rk
    unf_s[:, pl.ds(0, rows)] = (same & ((col & 15) == s)).astype(F32).astype(BF)
    for k in range(FOLD):
        hit = same & ((s >> 2) == k) & ((col & 15) == 12 + (s & 3))
        unf_s[:, pl.ds((k + 1) * rows, rows)] = hit.astype(F32).astype(BF)
    natural = 12 * zrow + 3 * jr + rk
    to_arrival = (iota((SLOTS, SLOTS), 1) == natural).astype(F32).astype(BF)

    for x in range(NX):
        h4[pl.ds(x * PAD + SLOTS, PAD - SLOTS), :] = jnp.zeros((PAD - SLOTS, H), BF)
    pltpu.make_async_copy(hid_hbm, hid_s, in_sem.at[3]).wait()
    mine = pl.ds(pl.multiple_of(ed * PAD, PAD), SLOTS)
    h4[mine, :] = dot(to_arrival, hid_s[...]).astype(BF)
    proj[...] = jnp.zeros_like(proj)
    pltpu.make_async_copy(og_s, og_s, in_sem.at[2]).wait()

    def fold(c):
        cols = pl.multiple_of(c * CH, CH)
        plain = dot(sel_s[pl.ds(0, rows), :], og_s[:, pl.ds(cols, 128 * FOLD)])
        last = og_s[:, pl.ds(pl.multiple_of(cols + 128 * FOLD, 128), 128)]
        for k in range(FOLD):
            part = plain[:, 128 * k : 128 * (k + 1)] + dot(sel_s[pl.ds((k + 1) * rows, rows), :], last)
            zs[c, :, pl.ds(128 * k, 128)] = part.astype(BF)

    z_mine = pl.ds(pl.multiple_of(z * ZROWS, ZROWS), ZROWS)

    def z_send(c):
        for h in OFFS:
            zt = at_z(h)
            theirs = pl.ds(pl.multiple_of(zt * ZROWS, ZROWS), ZROWS)
            remote(zs.at[c, theirs], zr.at[c, z_mine], zs_sem.at[c], zr_sem.at[c], to_z(zt)).start()
        pltpu.make_async_copy(zs.at[c, z_mine], zr.at[c, z_mine], zl_sem.at[c]).start()

    def z_copies(c):
        some = pl.ds(0, (NZ - 1) * ZROWS)
        return remote(zs.at[c, some], zr.at[c, some], zs_sem.at[c], zr_sem.at[c], to_z(z))

    fold(0)
    pl.semaphore_wait(barrier, NZ - 1 + 9)
    z_send(0)
    for h in range(1, NX):
        remote(h4.at[mine], h4.at[mine], hs_sem, hr_sem, {"edata": at_x(h)}).start()

    def first(c, carry):
        fold(c)
        z_send(c)
        return carry

    lax.fori_loop(1, LAG, first, 0)
    pltpu.make_async_copy(w_hbm, w_s, in_sem.at[4]).wait()

    j_mine = pl.ds(pl.multiple_of(j * PLANE_ROWS, PLANE_ROWS), PLANE_ROWS)

    def plane_copies(c):
        cols = pl.ds(pl.multiple_of(c * CH, CH), CH)
        some = pl.ds(0, (NJ - 1) * PLANE_ROWS)
        return remote(ps.at[c, some], ar.at[some, cols], ps_sem.at[c], pr_sem.at[c], to_j(j))

    def chunk(c):
        @pl.when(c + LAG < NCH)
        def _():
            z_copies(c).wait_send()
            fold(c + LAG)
            z_send(c + LAG)

        z_copies(c).wait_recv()
        pltpu.make_async_copy(zs.at[c, z_mine], zr.at[c, z_mine], zl_sem.at[c]).wait()
        ps[c, :, pl.ds(0, 128 * FOLD)] = dot(unf_s[:, pl.ds(0, rows)], zr[c]).astype(BF)
        stacked = jnp.concatenate([zr[c, :, pl.ds(128 * k, 128)] for k in range(FOLD)], axis=0)
        ps[c, :, pl.ds(128 * FOLD, 128)] = dot(unf_s[:, pl.ds(rows, FOLD * rows)], stacked).astype(BF)
        cols = pl.ds(pl.multiple_of(c * CH, CH), CH)
        for h in range(1, NJ):
            jt = at_j(h)
            theirs = pl.ds(pl.multiple_of(jt * PLANE_ROWS, PLANE_ROWS), PLANE_ROWS)
            remote(ps.at[c, theirs], ar.at[j_mine, cols], ps_sem.at[c], pr_sem.at[c], to_j(jt)).start()
        own = pltpu.make_async_copy(ps.at[c, j_mine], ar.at[j_mine, cols], pl_sem.at[c])
        own.start()
        own.wait()
        plane_copies(c).wait_recv()
        proj[...] += dot(ar[:, cols], w_s[cols, :])

    x_mine = pl.ds(pl.multiple_of(ed * PAD, PAD), PAD)

    def block_send(b):
        eye = (iota((128, 128), 0) == iota((128, 128), 1)).astype(F32).astype(BF)
        for g in range(BLK // 128):
            part = ar[:, pl.ds(pl.multiple_of(b * BLK + 128 * g, 128), 128)]
            part = jnp.concatenate([part, jnp.zeros((PAD - SLOTS, 128), BF)], axis=0)
            turned = lax.dot_general(eye, part, (((1,), (1,)), ((), ())), preferred_element_type=F32)
            xs[b, pl.ds(128 * g, 128), :] = turned.astype(BF)
        for h in range(1, NX):
            xt = at_x(h)
            theirs = pl.ds(pl.multiple_of(xt * OWN, 32), OWN)
            remote(xs.at[b, theirs], xr.at[b, :, x_mine], xs_sem.at[b], xr_sem.at[b], {"edata": xt}).start()
        theirs = pl.ds(pl.multiple_of(ed * OWN, 32), OWN)
        pltpu.make_async_copy(xs.at[b, theirs], xr.at[b, :, x_mine], xl_sem.at[b]).start()

    def x_copies(b):
        return remote(
            xs.at[b, pl.ds(0, (NX - 1) * OWN)], xr.at[b, :, pl.ds(0, (NX - 1) * PAD)],
            xs_sem.at[b], xr_sem.at[b], {"edata": ed},
        )

    def block_product(b):
        theirs = pl.ds(pl.multiple_of(ed * OWN, 32), OWN)
        pltpu.make_async_copy(xs.at[b, theirs], xr.at[b, :, x_mine], xl_sem.at[b]).wait()
        x_copies(b).wait_recv()
        return dot(xr[b], h4[...])

    def y_copy(b):
        step = jnp.where(b == 0, 2, jnp.where((b == 1) == (core == 0), 1, 3))
        return remote(ys.at[b], yr.at[b], ys_sem.at[b], yr_sem.at[b], {"dp": lax.rem(dp + step, NY)})

    def h_copies():
        some = pl.ds(0, (NX - 1) * SLOTS)
        return remote(h4.at[some], h4.at[some], hs_sem, hr_sem, {"edata": ed})

    def pair(b, carry):
        chunk(2 * b)
        chunk(2 * b + 1)
        block_send(b)

        @pl.when(b == 0)
        def _():
            h_copies().wait_recv()

        ys[b] = block_product(b).astype(BF)
        y_copy(b).start()
        return carry

    lax.fori_loop(0, NY - 1, pair, 0)
    chunk(NCH - 1)
    block_send(NY - 1)

    total = proj[...]
    slot_grad = jnp.sum(total * h4[mine, :].astype(F32), axis=1, keepdims=True)
    placed = jnp.where(iota((SLOTS, 128), 1) == 3 * j + rk, slot_grad, 0.0)
    gather = (iota((NZ, PLANE_ROWS), 0) == ((iota((NZ, PLANE_ROWS), 1) * 43) >> 7)).astype(F32)
    for jt in range(NJ):
        r1s[jt] = exact_dot(gather, placed[PLANE_ROWS * jt : PLANE_ROWS * (jt + 1)])
    for h in range(1, NJ):
        jt = at_j(h)
        remote(r1s.at[jt], r1r.at[j], r_sem.at[0], r_sem.at[1], to_j(jt)).start()
    r1_own = pltpu.make_async_copy(r1s.at[j], r1r.at[j], r_sem.at[2])
    r1_own.start()

    n = iota((SLOTS, 1), 0)
    nz = (n * 5462) >> 16
    rest = n - 12 * nz
    nj = (rest * 11) >> 5
    to_natural = (iota((SLOTS, SLOTS), 1) == 48 * nj + 3 * nz + (rest - 3 * nj)).astype(F32).astype(BF)
    gh_s[...] = dot(to_natural, total.astype(BF)).astype(BF)
    gh_out = pltpu.make_async_copy(gh_s, gh_hbm, out_sem.at[0])
    gh_out.start()

    r1_own.wait()
    r1_all = remote(r1s.at[pl.ds(0, NJ - 1)], r1r.at[pl.ds(0, NJ - 1)], r_sem.at[0], r_sem.at[1], to_j(j))
    r1_all.wait_recv()
    summed = r1r[0] + r1r[1] + r1r[2] + r1r[3]
    for zt in range(NZ):
        r2s[zt] = jnp.broadcast_to(summed[zt : zt + 1, :], (8, 128))
    for h in OFFS:
        zt = at_z(h)
        remote(r2s.at[zt], r2r.at[z], r_sem.at[3], r_sem.at[4], to_z(zt)).start()
    r2_own = pltpu.make_async_copy(r2s.at[z], r2r.at[z], r_sem.at[5])
    r2_own.start()

    down = block_product(NY - 1)
    for b in range(NY - 1):
        y_copy(b).wait_recv()
        down = down + yr[b].astype(F32)
    gd_s[...] = down.astype(BF)
    gd_out = pltpu.make_async_copy(gd_s, gd_hbm, out_sem.at[1])
    gd_out.start()

    r2_own.wait()
    r2_all = remote(r2s.at[pl.ds(0, NZ - 1)], r2r.at[pl.ds(0, NZ - 1)], r_sem.at[3], r_sem.at[4], to_z(z))
    r2_all.wait_recv()
    planes = jnp.concatenate([r2r[zt, pl.ds(0, 1), :] for zt in range(NZ)], axis=0)
    experts = NZ * NJ
    spread = (iota((experts, NZ), 0) >> 2 == iota((experts, NZ), 1)).astype(F32)
    row = exact_dot(spread, planes)
    e_lane = 3 * (iota((experts, 1), 0) & 3)
    lane = iota((experts, 128), 1)
    grads = jnp.zeros((experts, TOK), F32)
    for r in range(CAP):
        value = jnp.sum(jnp.where(lane == e_lane + r, row, 0.0), axis=1, keepdims=True)
        grads = grads + jnp.where((cnt_s[...] > 0.0) & (rank_s[...] == float(r)), value, 0.0)
    ids = ids_s[...]
    scores = jax.nn.sigmoid(logit_s[...])
    score_sum = jnp.sum(scores, axis=0, keepdims=True)
    weights = (2.5 * scores / score_sum).astype(BF).astype(F32)
    e_col = iota((experts, 1), 0)
    picked = [
        jnp.sum(jnp.where(ids[k : k + 1, :] == e_col, grads, 0.0), axis=0, keepdims=True) for k in range(TOP)
    ]
    combine_grad = jnp.concatenate(picked, axis=0) / weights
    mean = jnp.sum(combine_grad * scores, axis=0, keepdims=True) / score_sum
    lg_s[...] = scores * (1.0 - scores) * (2.5 / score_sum) * (combine_grad - mean)
    lg_out = pltpu.make_async_copy(lg_s, lg_hbm, out_sem.at[2])
    lg_out.start()

    h_copies().wait_send()

    def drain_z(c, carry):
        z_copies(c).wait_send()
        return carry

    def drain_p(c, carry):
        plane_copies(c).wait_send()
        return carry

    def drain_x(b, carry):
        x_copies(b).wait_send()
        return carry

    def drain_y(b, carry):
        y_copy(b).wait_send()
        return carry

    lax.fori_loop(NCH - LAG, NCH, drain_z, 0)
    lax.fori_loop(0, NCH, drain_p, 0)
    lax.fori_loop(0, NY, drain_x, 0)
    lax.fori_loop(0, NY - 1, drain_y, 0)
    r1_all.wait_send()
    r2_all.wait_send()
    gh_out.wait()
    gd_out.wait()
    lg_out.wait()


def on_device(out_grad, route_ids, router_logits, hidden, down_weight):
    rows = NZ * ZROWS
    dma = pltpu.SemaphoreType.DMA
    vm = pltpu.VMEM
    anywhere = pl.BlockSpec(memory_space=pl.ANY)
    grad_down, grad_hidden, logit_grad = pl.pallas_call(
        kernel,
        out_shape=(
            jax.ShapeDtypeStruct((OWN, H), BF),
            jax.ShapeDtypeStruct((SLOTS, H), BF),
            jax.ShapeDtypeStruct((TOP, TOK), F32),
        ),
        in_specs=[anywhere] * 5,
        out_specs=(anywhere,) * 3,
        scratch_shapes=[
            vm((2 * TOK, D), BF), vm((TOP, TOK), jnp.int32), vm((TOP, TOK), F32), vm((SLOTS, H), BF), vm((D, H), BF),
            vm(((1 + FOLD) * rows, 2 * TOK), BF), vm((SLOTS, (1 + FOLD) * rows), BF), vm((NX * PAD, H), BF),
            vm((NCH, rows, 128 * FOLD), BF), vm((NCH, rows, 128 * FOLD), BF), vm((NCH, SLOTS, CH), BF), vm((SLOTS, D), BF),
            vm((NY, BLK, PAD), BF), vm((NY, OWN, NX * PAD), BF), vm((NY - 1, OWN, H), BF), vm((NY - 1, OWN, H), BF),
            vm((SLOTS, H), F32), vm((NZ * NJ, TOK), F32), vm((NZ * NJ, TOK), F32),
            vm((NJ, NZ, 128), F32), vm((NJ, NZ, 128), F32), vm((NZ, 8, 128), F32), vm((NZ, 8, 128), F32),
            vm((OWN, H), BF), vm((SLOTS, H), BF), vm((TOP, TOK), F32),
            dma((5,)), dma((3,)), dma, dma, dma((NCH,)), dma((NCH,)), dma((NCH,)), dma((NCH,)), dma((NCH,)), dma((NCH,)),
            dma((NY,)), dma((NY,)), dma((NY,)), dma((NY - 1,)), dma((NY - 1,)), dma((6,)),
        ],
        compiler_params=pltpu.CompilerParams(
            collective_id=0, has_side_effects=True, vmem_limit_bytes=52 << 20
        ),
        cost_estimate=pl.CostEstimate(flops=4 * SLOTS * D * H, bytes_accessed=2 * D * H, transcendentals=0),
    )(
        out_grad,
        route_ids.T,
        router_logits.T,
        hidden.reshape(SLOTS, H),
        down_weight.reshape(D, H),
    )
    return grad_down.reshape(OWN, 1, H), grad_hidden.reshape(1, 1, SLOTS, H), logit_grad.T


def solution(mesh):
    in_specs = (
        P(("dp", "edata", "expert"), None),
        P(("dp", "edata", "expert"), None),
        P(("dp", "edata", "expert"), None),
        P(("dp", "edata"), "expert", None, None),
        P(None, "expert", None),
    )
    out_specs = (
        P(("dp", "edata"), "expert", None),
        P(("dp", "edata"), "expert", None, None),
        P(("dp", "edata", "expert"), None),
    )
    return jax.shard_map(
        on_device, mesh=mesh, in_specs=in_specs, out_specs=out_specs, check_vma=False
    )
```

```python
import jax
import jax.numpy as jnp
from jax import lax
from jax.experimental import pallas as pl
from jax.experimental.pallas import tpu as pltpu
from jax.sharding import PartitionSpec as P

MESH = pl.DeviceIdType.MESH
BF = jnp.bfloat16
F32 = jnp.float32
NZ = 16
NJ = 4
NX = 4
NY = 4
CAP = 3
TOK = 128
TOP = 8
D = 3584
H = 1024
SLOTS = NZ * NJ * CAP
PLANE_ROWS = NZ * CAP
ZROWS = 16
CH = 512
NCH = D // CH
FOLD = CH // 128 - 1
BLK = D // NY
OWN = BLK // NX
PAD = 256
OFFS = [8, 7, 9, 6, 10, 5, 11, 4, 12, 3, 13, 2, 14, 1, 15]


def iota(shape, axis):
    return lax.broadcasted_iota(jnp.int32, shape, axis)


def dot(a, b):
    return jnp.dot(a, b, preferred_element_type=F32)


def exact_dot(a, b):
    return jnp.dot(a, b, preferred_element_type=F32, precision=lax.Precision.HIGHEST)


def third(q):
    return (q * 11) >> 5


def send_parts(row):
    j = (row * 1366) >> 16
    rest = row - PLANE_ROWS * j
    z = (rest * 43) >> 7
    return j, z, rest - 3 * z


def folded_slot(row, part):
    q = row & 15
    if part == 0:
        return jnp.where(q < 12, q, -1)
    return jnp.where(q >= 12, 4 * (part - 1) + (q - 12), -1)


def one_hot(mask):
    return mask.astype(F32).astype(BF)


def named(ids, weights, expert):
    rows = expert.shape[0]
    count = jnp.zeros((rows, TOK), F32)
    weight = jnp.zeros((rows, TOK), F32)
    for k in range(TOP):
        hit = ids[k : k + 1, :] == expert
        count = count + jnp.where(hit, 1.0, 0.0)
        weight = weight + jnp.where(hit, weights[k : k + 1, :], 0.0)
    before = (iota((TOK, TOK), 0) < iota((TOK, TOK), 1)).astype(F32).astype(BF)
    rank = dot(count.astype(BF), before)
    return count, weight, rank


def kernel(
    og_hbm, ids_hbm, logit_hbm, hid_hbm, w_hbm,
    gd_hbm, gh_hbm, lg_hbm,
    og_s, ids_s, logit_s, w_s, sel_s, fold_s, unf_s, h4, zs, zr, ps, pr, ar, xs, xr, ys, yr, proj,
    cnt_s, rank_s, r1s, r1r, r2r, gd_s, gh_s, lg_s,
    in_sem, out_sem, hs_sem, hr_sem, zs_sem, zr_sem, zl_sem, ps_sem, pr_sem, pl_sem,
    xs_sem, xr_sem, xl_sem, ys_sem, yr_sem, r_sem,
):
    dp = lax.axis_index("dp")
    ed = lax.axis_index("edata")
    ex = lax.axis_index("expert")
    z = ex // NJ
    j = ex % NJ
    core = ex % 2

    def at_z(h):
        return lax.rem(z + h, NZ)

    def at_j(h):
        return lax.rem(j + h, NJ)

    def at_x(h):
        return lax.rem(ed + h, NX)

    def to_z(zt):
        return {"expert": zt * NJ + j}

    def to_j(jt):
        return {"expert": z * NJ + jt}

    def owner(b, c):
        step = (2, 1, 3, 0)[b] if not isinstance(c, int) else ((2, 1, 3, 0), (2, 3, 1, 0))[c][b]
        if not isinstance(c, int) and b in (1, 2):
            step = jnp.where(c == 0, step, 4 - step)
        return lax.rem(dp + step, NY)

    def remote(src, dst, ssem, rsem, where):
        return pltpu.make_async_remote_copy(
            src_ref=src, dst_ref=dst, send_sem=ssem, recv_sem=rsem, device_id=where, device_id_type=MESH
        )

    barrier = pltpu.get_barrier_semaphore()
    for h in OFFS:
        pl.semaphore_signal(barrier, inc=1, device_id=to_z(at_z(h)), device_id_type=MESH)
    for h in range(1, 4):
        pl.semaphore_signal(barrier, inc=1, device_id=to_j(at_j(h)), device_id_type=MESH)
        pl.semaphore_signal(barrier, inc=1, device_id={"edata": at_x(h)}, device_id_type=MESH)
        pl.semaphore_signal(barrier, inc=1, device_id={"dp": lax.rem(dp + h, NY)}, device_id_type=MESH)

    pltpu.make_async_copy(ids_hbm, ids_s, in_sem.at[0]).start()
    pltpu.make_async_copy(logit_hbm, logit_s, in_sem.at[1]).start()
    for c in range(2):
        for b in range(NY):
            start = pl.multiple_of(owner(b, c) * BLK, BLK)
            pltpu.make_async_copy(
                og_hbm.at[:, pl.ds(start, BLK)],
                og_s.at[pl.ds(c * TOK, TOK), pl.ds(b * BLK, BLK)],
                in_sem.at[2],
            ).start()
    pltpu.make_async_copy(hid_hbm, h4.at[pl.ds(pl.multiple_of(ed * PAD, PAD), SLOTS)], in_sem.at[3]).start()
    for b in range(NY):
        start = pl.multiple_of(owner(b, core) * BLK, BLK)
        pltpu.make_async_copy(
            w_hbm.at[pl.ds(start, BLK)], w_s.at[pl.ds(b * BLK, BLK)], in_sem.at[4]
        ).start()

    pltpu.make_async_copy(ids_hbm, ids_s, in_sem.at[0]).wait()
    pltpu.make_async_copy(logit_hbm, logit_s, in_sem.at[1]).wait()
    ids = ids_s[...]
    scores = jax.nn.sigmoid(logit_s[...])
    score_sum = jnp.sum(scores, axis=0, keepdims=True)
    weights = (2.5 * scores / score_sum).astype(BF).astype(F32)
    rows = NZ * ZROWS
    jt, zt, rank_of = send_parts(iota((SLOTS, 1), 0))
    count, weight, rank = named(ids, weights, zt * NJ + jt)
    chosen = jnp.where((count > 0.0) & (rank == rank_of.astype(F32)), weight, 0.0)
    odd = (jt & 1) == 1
    sel_s[:, pl.ds(0, TOK)] = jnp.where(odd, 0.0, chosen).astype(BF)
    sel_s[:, pl.ds(TOK, TOK)] = jnp.where(odd, chosen, 0.0).astype(BF)
    pltpu.make_async_copy(og_s, og_s, in_sem.at[2]).wait()

    z_mine = pl.ds(pl.multiple_of(z * ZROWS, ZROWS), ZROWS)
    j_mine = pl.ds(pl.multiple_of(j * PLANE_ROWS, PLANE_ROWS), PLANE_ROWS)

    def select(c):
        cols = pl.ds(pl.multiple_of(c * CH, CH), CH)
        ps[c] = dot(sel_s[...], og_s[:, cols]).astype(BF)

    def plane_send(c):
        for h in range(1, NJ):
            to = at_j(h)
            theirs = pl.ds(pl.multiple_of(to * PLANE_ROWS, PLANE_ROWS), PLANE_ROWS)
            remote(ps.at[c, theirs], pr.at[c, j_mine], ps_sem.at[c], pr_sem.at[c], to_j(to)).start()
        pltpu.make_async_copy(ps.at[c, j_mine], pr.at[c, j_mine], pl_sem.at[c]).start()

    def plane_copies(c):
        some = pl.ds(0, (NJ - 1) * PLANE_ROWS)
        return remote(ps.at[c, some], pr.at[c, some], ps_sem.at[c], pr_sem.at[c], to_j(j))

    def fold(c):
        plain = dot(fold_s[pl.ds(0, rows), :], pr[c, :, pl.ds(0, 128 * FOLD)])
        last = dot(fold_s[pl.ds(rows, FOLD * rows), :], pr[c, :, pl.ds(128 * FOLD, 128)])
        for k in range(FOLD):
            part = plain[:, 128 * k : 128 * (k + 1)] + last[rows * k : rows * (k + 1)]
            zs[c, :, pl.ds(128 * k, 128)] = part.astype(BF)

    def z_send(c):
        for h in OFFS:
            to = at_z(h)
            theirs = pl.ds(pl.multiple_of(to * ZROWS, ZROWS), ZROWS)
            remote(zs.at[c, theirs], zr.at[c, z_mine], zs_sem.at[c], zr_sem.at[c], to_z(to)).start()
        pltpu.make_async_copy(zs.at[c, z_mine], zr.at[c, z_mine], zl_sem.at[c]).start()

    def z_copies(c):
        some = pl.ds(0, (NZ - 1) * ZROWS)
        return remote(zs.at[c, some], zr.at[c, some], zs_sem.at[c], zr_sem.at[c], to_z(z))

    def select_loop(c, carry):
        select(c)
        return carry

    lax.fori_loop(0, NCH, select_loop, 0)

    row = iota((rows, 1), 0)
    cj, cz, crank = send_parts(iota((rows, SLOTS), 1))
    for part in range(1 + FOLD):
        slot = folded_slot(row, part)
        fold_s[pl.ds(part * rows, rows), :] = one_hot((cz == (row >> 4)) & (3 * cj + crank == slot))
    n = iota((SLOTS, 1), 0)
    nz = (n * 5462) >> 16
    col = iota((SLOTS, rows), 1)
    for part in range(1 + FOLD):
        slot = folded_slot(col, part)
        unf_s[:, pl.ds(part * rows, rows)] = one_hot(((col >> 4) == nz) & (n - 12 * nz == slot))

    for x in range(NX):
        h4[pl.ds(x * PAD + SLOTS, PAD - SLOTS), :] = jnp.zeros((PAD - SLOTS, H), BF)
    mine = pl.ds(pl.multiple_of(ed * PAD, PAD), SLOTS)
    pltpu.make_async_copy(hid_hbm, h4.at[mine], in_sem.at[3]).wait()
    proj[...] = jnp.zeros_like(proj)
    count, _, rank = named(ids, weights, iota((NZ * NJ, 1), 0))
    cnt_s[...] = count
    rank_s[...] = rank

    pl.semaphore_wait(barrier, NZ - 1 + 9)

    def plane_loop(c, carry):
        plane_send(c)
        return carry

    lax.fori_loop(0, NCH, plane_loop, 0)
    for h in range(1, NX):
        remote(h4.at[mine], h4.at[mine], hs_sem, hr_sem, {"edata": at_x(h)}).start()

    def fold_loop(c, carry):
        pltpu.make_async_copy(ps.at[c, j_mine], pr.at[c, j_mine], pl_sem.at[c]).wait()
        plane_copies(c).wait_recv()
        fold(c)
        z_send(c)
        return carry

    lax.fori_loop(0, NCH, fold_loop, 0)
    pltpu.make_async_copy(w_hbm, w_s, in_sem.at[4]).wait()

    def chunk(c):
        z_copies(c).wait_recv()
        pltpu.make_async_copy(zs.at[c, z_mine], zr.at[c, z_mine], zl_sem.at[c]).wait()
        first = pl.multiple_of(c * CH, CH)
        ar[:, pl.ds(first, 128 * FOLD)] = dot(unf_s[:, pl.ds(0, rows)], zr[c]).astype(BF)
        stacked = jnp.concatenate([zr[c, :, pl.ds(128 * k, 128)] for k in range(FOLD)], axis=0)
        last = pl.ds(pl.multiple_of(first + 128 * FOLD, 128), 128)
        ar[:, last] = dot(unf_s[:, pl.ds(rows, FOLD * rows)], stacked).astype(BF)

    def project(c):
        cols = pl.ds(pl.multiple_of(c * CH, CH), CH)
        proj[...] += dot(ar[:, cols], w_s[cols, :])

    x_mine = pl.ds(pl.multiple_of(ed * PAD, PAD), PAD)

    def block_send(b):
        eye = (iota((128, 128), 0) == iota((128, 128), 1)).astype(F32).astype(BF)
        for g in range(BLK // 128):
            part = ar[:, pl.ds(pl.multiple_of(b * BLK + 128 * g, 128), 128)]
            part = jnp.concatenate([part, jnp.zeros((PAD - SLOTS, 128), BF)], axis=0)
            turned = lax.dot_general(eye, part, (((1,), (1,)), ((), ())), preferred_element_type=F32)
            xs[b, pl.ds(128 * g, 128), :] = turned.astype(BF)
        for h in range(1, NX):
            xt = at_x(h)
            theirs = pl.ds(pl.multiple_of(xt * OWN, 32), OWN)
            remote(xs.at[b, theirs], xr.at[b, :, x_mine], xs_sem.at[b], xr_sem.at[b], {"edata": xt}).start()
        theirs = pl.ds(pl.multiple_of(ed * OWN, 32), OWN)
        pltpu.make_async_copy(xs.at[b, theirs], xr.at[b, :, x_mine], xl_sem.at[b]).start()

    def x_copies(b):
        return remote(
            xs.at[b, pl.ds(0, (NX - 1) * OWN)], xr.at[b, :, pl.ds(0, (NX - 1) * PAD)],
            xs_sem.at[b], xr_sem.at[b], {"edata": ed},
        )

    def block_product(b):
        theirs = pl.ds(pl.multiple_of(ed * OWN, 32), OWN)
        pltpu.make_async_copy(xs.at[b, theirs], xr.at[b, :, x_mine], xl_sem.at[b]).wait()
        x_copies(b).wait_recv()
        return dot(xr[b], h4[...])

    def y_copy(b):
        step = jnp.where(b == 0, 2, jnp.where((b == 1) == (core == 0), 1, 3))
        return remote(ys.at[b], yr.at[b], ys_sem.at[b], yr_sem.at[b], {"dp": lax.rem(dp + step, NY)})

    def h_copies():
        some = pl.ds(0, (NX - 1) * SLOTS)
        return remote(h4.at[some], h4.at[some], hs_sem, hr_sem, {"edata": ed})

    def pair(b, carry):
        chunk(2 * b)
        project(2 * b)
        chunk(2 * b + 1)
        block_send(b)
        project(2 * b + 1)

        @pl.when(b == 0)
        def _():
            h_copies().wait_recv()

        ys[b] = block_product(b).astype(BF)
        y_copy(b).start()
        return carry

    lax.fori_loop(0, NY - 1, pair, 0)
    chunk(NCH - 1)
    block_send(NY - 1)
    project(NCH - 1)

    total = proj[...]
    slot_grad = jnp.sum(total * h4[mine, :].astype(F32), axis=1, keepdims=True)
    placed = jnp.where(iota((SLOTS, 128), 1) == n - 12 * nz, slot_grad, 0.0)
    gather = (iota((NZ, SLOTS), 0) == ((iota((NZ, SLOTS), 1) * 5462) >> 16)).astype(F32)
    by_plane = exact_dot(gather, placed)
    for to in range(NZ):
        r1s[to] = jnp.broadcast_to(by_plane[to : to + 1, :], (8, 128))
    for h in OFFS:
        to = at_z(h)
        remote(r1s.at[to], r1r.at[z], r_sem.at[0], r_sem.at[1], to_z(to)).start()
    r1_own = pltpu.make_async_copy(r1s.at[z], r1r.at[z], r_sem.at[2])
    r1_own.start()
    gh_s[...] = total.astype(BF)
    gh_out = pltpu.make_async_copy(gh_s, gh_hbm, out_sem.at[0])
    gh_out.start()
    r1_own.wait()
    r1_all = remote(r1s.at[pl.ds(0, NZ - 1)], r1r.at[pl.ds(0, NZ - 1)], r_sem.at[0], r_sem.at[1], to_z(z))
    r1_all.wait_recv()
    planes = jnp.concatenate([r1r[zt, pl.ds(0, 1), :] for zt in range(NZ)], axis=0)
    j_rows = pl.ds(pl.multiple_of(j * NZ, NZ), NZ)
    r2r[j_rows, :] = planes
    for h in range(1, NJ):
        remote(r2r.at[j_rows], r2r.at[j_rows], r_sem.at[3], r_sem.at[4], to_j(at_j(h))).start()

    down = block_product(NY - 1)
    for b in range(NY - 1):
        y_copy(b).wait_recv()
        down = down + yr[b].astype(F32)
    gd_s[...] = down.astype(BF)
    gd_out = pltpu.make_async_copy(gd_s, gd_hbm, out_sem.at[1])
    gd_out.start()

    some = pl.ds(0, (NJ - 1) * NZ)
    r2_all = remote(r2r.at[some], r2r.at[some], r_sem.at[3], r_sem.at[4], to_j(j))
    r2_all.wait_recv()
    experts = NZ * NJ
    e_row = iota((experts, experts), 0)
    spread = (iota((experts, experts), 1) == (e_row & 3) * NZ + (e_row >> 2)).astype(F32)
    values = exact_dot(spread, r2r[...])
    lane = iota((experts, 128), 1) - 3 * j
    grads = jnp.zeros((experts, TOK), F32)
    for r in range(CAP):
        value = jnp.sum(jnp.where(lane == r, values, 0.0), axis=1, keepdims=True)
        grads = grads + jnp.where((cnt_s[...] > 0.0) & (rank_s[...] == float(r)), value, 0.0)
    ids = ids_s[...]
    scores = jax.nn.sigmoid(logit_s[...])
    score_sum = jnp.sum(scores, axis=0, keepdims=True)
    weights = (2.5 * scores / score_sum).astype(BF).astype(F32)
    e_col = iota((experts, 1), 0)
    picked = [
        jnp.sum(jnp.where(ids[k : k + 1, :] == e_col, grads, 0.0), axis=0, keepdims=True) for k in range(TOP)
    ]
    combine_grad = jnp.concatenate(picked, axis=0) / weights
    mean = jnp.sum(combine_grad * scores, axis=0, keepdims=True) / score_sum
    lg_s[...] = scores * (1.0 - scores) * (2.5 / score_sum) * (combine_grad - mean)
    lg_out = pltpu.make_async_copy(lg_s, lg_hbm, out_sem.at[2])
    lg_out.start()

    h_copies().wait_send()

    def drain_z(c, carry):
        z_copies(c).wait_send()
        return carry

    def drain_p(c, carry):
        plane_copies(c).wait_send()
        return carry

    def drain_x(b, carry):
        x_copies(b).wait_send()
        return carry

    def drain_y(b, carry):
        y_copy(b).wait_send()
        return carry

    lax.fori_loop(0, NCH, drain_z, 0)
    lax.fori_loop(0, NCH, drain_p, 0)
    lax.fori_loop(0, NY, drain_x, 0)
    lax.fori_loop(0, NY - 1, drain_y, 0)
    r1_all.wait_send()
    r2_all.wait_send()
    gh_out.wait()
    gd_out.wait()
    lg_out.wait()


def on_device(out_grad, route_ids, router_logits, hidden, down_weight):
    rows = NZ * ZROWS
    dma = pltpu.SemaphoreType.DMA
    vm = pltpu.VMEM
    anywhere = pl.BlockSpec(memory_space=pl.ANY)
    grad_down, grad_hidden, logit_grad = pl.pallas_call(
        kernel,
        out_shape=(
            jax.ShapeDtypeStruct((OWN, H), BF),
            jax.ShapeDtypeStruct((SLOTS, H), BF),
            jax.ShapeDtypeStruct((TOP, TOK), F32),
        ),
        in_specs=[anywhere] * 5,
        out_specs=(anywhere,) * 3,
        scratch_shapes=[
            vm((2 * TOK, D), BF), vm((TOP, TOK), jnp.int32), vm((TOP, TOK), F32), vm((D, H), BF),
            vm((SLOTS, 2 * TOK), BF), vm(((1 + FOLD) * rows, SLOTS), BF), vm((SLOTS, (1 + FOLD) * rows), BF), vm((NX * PAD, H), BF),
            vm((NCH, rows, 128 * FOLD), BF), vm((NCH, rows, 128 * FOLD), BF), vm((NCH, SLOTS, CH), BF), vm((NCH, SLOTS, CH), BF), vm((SLOTS, D), BF),
            vm((NY, BLK, PAD), BF), vm((NY, OWN, NX * PAD), BF), vm((NY - 1, OWN, H), BF), vm((NY - 1, OWN, H), BF),
            vm((SLOTS, H), F32), vm((NZ * NJ, TOK), F32), vm((NZ * NJ, TOK), F32),
            vm((NZ, 8, 128), F32), vm((NZ, 8, 128), F32), vm((NJ * NZ, 128), F32),
            vm((OWN, H), BF), vm((SLOTS, H), BF), vm((TOP, TOK), F32),
            dma((5,)), dma((3,)), dma, dma, dma((NCH,)), dma((NCH,)), dma((NCH,)), dma((NCH,)), dma((NCH,)), dma((NCH,)),
            dma((NY,)), dma((NY,)), dma((NY,)), dma((NY - 1,)), dma((NY - 1,)), dma((6,)),
        ],
        compiler_params=pltpu.CompilerParams(
            collective_id=0, has_side_effects=True, vmem_limit_bytes=62 << 20
        ),
        cost_estimate=pl.CostEstimate(flops=4 * SLOTS * D * H, bytes_accessed=2 * D * H, transcendentals=0),
    )(
        out_grad,
        route_ids.T,
        router_logits.T,
        hidden.reshape(SLOTS, H),
        down_weight.reshape(D, H),
    )
    return grad_down.reshape(OWN, 1, H), grad_hidden.reshape(1, 1, SLOTS, H), logit_grad.T


def solution(mesh):
    in_specs = (
        P(("dp", "edata", "expert"), None),
        P(("dp", "edata", "expert"), None),
        P(("dp", "edata", "expert"), None),
        P(("dp", "edata"), "expert", None, None),
        P(None, "expert", None),
    )
    out_specs = (
        P(("dp", "edata"), "expert", None),
        P(("dp", "edata"), "expert", None, None),
        P(("dp", "edata", "expert"), None),
    )
    return jax.shard_map(
        on_device, mesh=mesh, in_specs=in_specs, out_specs=out_specs, check_vma=False
    )
```

```python
import jax
import jax.numpy as jnp
from jax import lax
from jax.experimental import pallas as pl
from jax.experimental.pallas import tpu as pltpu
from jax.sharding import PartitionSpec as P

MESH = pl.DeviceIdType.MESH
BF = jnp.bfloat16
F32 = jnp.float32
NZ = 16
NJ = 4
NX = 4
NY = 4
CAP = 3
TOK = 128
TOP = 8
D = 3584
H = 1024
SLOTS = NZ * NJ * CAP
PLANE_ROWS = NZ * CAP
ZROWS = 16
CH = 512
NCH = D // CH
FOLD = CH // 128 - 1
BLK = D // NY
OWN = BLK // NX
PAD = 256
SPLIT = (BLK * (NY - 1)) // CH
OFFS = [8, 7, 9, 6, 10, 5, 11, 4, 12, 3, 13, 2, 14, 1, 15]


def iota(shape, axis):
    return lax.broadcasted_iota(jnp.int32, shape, axis)


def dot(a, b):
    return jnp.dot(a, b, preferred_element_type=F32)


def exact_dot(a, b):
    return jnp.dot(a, b, preferred_element_type=F32, precision=lax.Precision.HIGHEST)


def third(q):
    return (q * 11) >> 5


def send_parts(row):
    j = (row * 1366) >> 16
    rest = row - PLANE_ROWS * j
    z = (rest * 43) >> 7
    return j, z, rest - 3 * z


def folded_slot(row, part):
    q = row & 15
    if part == 0:
        return jnp.where(q < 12, q, -1)
    return jnp.where(q >= 12, 4 * (part - 1) + (q - 12), -1)


def one_hot(mask):
    return mask.astype(F32).astype(BF)


def named(ids, weights, expert):
    rows = expert.shape[0]
    count = jnp.zeros((rows, TOK), F32)
    weight = jnp.zeros((rows, TOK), F32)
    for k in range(TOP):
        hit = ids[k : k + 1, :] == expert
        count = count + jnp.where(hit, 1.0, 0.0)
        weight = weight + jnp.where(hit, weights[k : k + 1, :], 0.0)
    before = (iota((TOK, TOK), 0) < iota((TOK, TOK), 1)).astype(F32).astype(BF)
    rank = dot(count.astype(BF), before)
    return count, weight, rank


def kernel(
    og_hbm, ids_hbm, logit_hbm, hid_hbm, w_hbm,
    gd_hbm, gh_hbm, lg_hbm,
    og_s, ids_s, logit_s, w_s, sel_s, fold_s, unf_s, h4, zs, zr, ps, pr, ar, xs, xr, ys, yr, proj,
    cnt_s, rank_s, r1s, r1r, r2r, gd_s, gh_s, lg_s,
    in_sem, out_sem, hs_sem, hr_sem, zs_sem, zr_sem, zl_sem, ps_sem, pr_sem, pl_sem,
    xs_sem, xr_sem, xl_sem, ys_sem, yr_sem, r_sem,
):
    dp = lax.axis_index("dp")
    ed = lax.axis_index("edata")
    ex = lax.axis_index("expert")
    z = ex // NJ
    j = ex % NJ
    core = ex % 2

    def at_z(h):
        return lax.rem(z + h, NZ)

    def at_j(h):
        return lax.rem(j + h, NJ)

    def at_x(h):
        return lax.rem(ed + h, NX)

    def to_z(zt):
        return {"expert": zt * NJ + j}

    def to_j(jt):
        return {"expert": z * NJ + jt}

    def owner(b, c):
        step = (2, 1, 3, 0)[b] if not isinstance(c, int) else ((2, 1, 3, 0), (2, 3, 1, 0))[c][b]
        if not isinstance(c, int) and b in (1, 2):
            step = jnp.where(c == 0, step, 4 - step)
        return lax.rem(dp + step, NY)

    def remote(src, dst, ssem, rsem, where):
        return pltpu.make_async_remote_copy(
            src_ref=src, dst_ref=dst, send_sem=ssem, recv_sem=rsem, device_id=where, device_id_type=MESH
        )

    barrier = pltpu.get_barrier_semaphore()
    for h in OFFS:
        pl.semaphore_signal(barrier, inc=1, device_id=to_z(at_z(h)), device_id_type=MESH)
    for h in range(1, 4):
        pl.semaphore_signal(barrier, inc=1, device_id=to_j(at_j(h)), device_id_type=MESH)
        pl.semaphore_signal(barrier, inc=1, device_id={"edata": at_x(h)}, device_id_type=MESH)
        pl.semaphore_signal(barrier, inc=1, device_id={"dp": lax.rem(dp + h, NY)}, device_id_type=MESH)

    pltpu.make_async_copy(ids_hbm, ids_s, in_sem.at[0]).start()
    pltpu.make_async_copy(logit_hbm, logit_s, in_sem.at[1]).start()
    for c in range(2):
        for b in range(NY):
            start = pl.multiple_of(owner(b, c) * BLK, BLK)
            pltpu.make_async_copy(
                og_hbm.at[:, pl.ds(start, BLK)],
                og_s.at[pl.ds(c * TOK, TOK), pl.ds(b * BLK, BLK)],
                in_sem.at[2],
            ).start()
    pltpu.make_async_copy(hid_hbm, h4.at[pl.ds(pl.multiple_of(ed * PAD, PAD), SLOTS)], in_sem.at[3]).start()
    for b in range(NY):
        start = pl.multiple_of(owner(b, core) * BLK, BLK)
        pltpu.make_async_copy(
            w_hbm.at[pl.ds(start, BLK)], w_s.at[pl.ds(b * BLK, BLK)], in_sem.at[4]
        ).start()

    pltpu.make_async_copy(ids_hbm, ids_s, in_sem.at[0]).wait()
    pltpu.make_async_copy(logit_hbm, logit_s, in_sem.at[1]).wait()
    ids = ids_s[...]
    scores = jax.nn.sigmoid(logit_s[...])
    score_sum = jnp.sum(scores, axis=0, keepdims=True)
    weights = (2.5 * scores / score_sum).astype(BF).astype(F32)
    rows = NZ * ZROWS
    jt, zt, rank_of = send_parts(iota((SLOTS, 1), 0))
    count, weight, rank = named(ids, weights, zt * NJ + jt)
    chosen = jnp.where((count > 0.0) & (rank == rank_of.astype(F32)), weight, 0.0)
    odd = (jt & 1) == 1
    sel_s[:, pl.ds(0, TOK)] = jnp.where(odd, 0.0, chosen).astype(BF)
    sel_s[:, pl.ds(TOK, TOK)] = jnp.where(odd, chosen, 0.0).astype(BF)
    pltpu.make_async_copy(og_s, og_s, in_sem.at[2]).wait()

    z_mine = pl.ds(pl.multiple_of(z * ZROWS, ZROWS), ZROWS)
    j_mine = pl.ds(pl.multiple_of(j * PLANE_ROWS, PLANE_ROWS), PLANE_ROWS)

    def select(c):
        cols = pl.ds(pl.multiple_of(c * CH, CH), CH)
        ps[c] = dot(sel_s[...], og_s[:, cols]).astype(BF)

    def plane_send(c):
        for h in range(1, NJ):
            to = at_j(h)
            theirs = pl.ds(pl.multiple_of(to * PLANE_ROWS, PLANE_ROWS), PLANE_ROWS)
            remote(ps.at[c, theirs], pr.at[c, j_mine], ps_sem.at[c], pr_sem.at[c], to_j(to)).start()
        pltpu.make_async_copy(ps.at[c, j_mine], pr.at[c, j_mine], pl_sem.at[c]).start()

    def plane_copies(c):
        some = pl.ds(0, (NJ - 1) * PLANE_ROWS)
        return remote(ps.at[c, some], pr.at[c, some], ps_sem.at[c], pr_sem.at[c], to_j(j))

    def fold(c):
        plain = dot(fold_s[pl.ds(0, rows), :], pr[c, :, pl.ds(0, 128 * FOLD)])
        last = dot(fold_s[pl.ds(rows, FOLD * rows), :], pr[c, :, pl.ds(128 * FOLD, 128)])
        for k in range(FOLD):
            part = plain[:, 128 * k : 128 * (k + 1)] + last[rows * k : rows * (k + 1)]
            zs[c, :, pl.ds(128 * k, 128)] = part.astype(BF)

    def z_send(c, first=0, width=128 * FOLD, at=None):
        at = c if at is None else at
        part = pl.ds(first, width)
        for h in OFFS:
            to = at_z(h)
            theirs = pl.ds(pl.multiple_of(to * ZROWS, ZROWS), ZROWS)
            remote(
                zs.at[c, theirs, part], zr.at[c, z_mine, part], zs_sem.at[at], zr_sem.at[at], to_z(to)
            ).start()

    def z_own(c):
        return pltpu.make_async_copy(zs.at[c, z_mine], zr.at[c, z_mine], zl_sem.at[c])

    def z_copies(c, first=0, width=128 * FOLD, at=None):
        at = c if at is None else at
        some, part = pl.ds(0, (NZ - 1) * ZROWS), pl.ds(first, width)
        return remote(zs.at[c, some, part], zr.at[c, some, part], zs_sem.at[at], zr_sem.at[at], to_z(z))

    select(0)
    pl.semaphore_wait(barrier, NZ - 1 + 9)
    plane_send(0)
    select(1)
    plane_send(1)

    row = iota((rows, 1), 0)
    cj, cz, crank = send_parts(iota((rows, SLOTS), 1))
    for part in range(1 + FOLD):
        slot = folded_slot(row, part)
        fold_s[pl.ds(part * rows, rows), :] = one_hot((cz == (row >> 4)) & (3 * cj + crank == slot))
    def fold_and_send(c):
        pltpu.make_async_copy(ps.at[c, j_mine], pr.at[c, j_mine], pl_sem.at[c]).wait()
        plane_copies(c).wait_recv()
        fold(c)
        z_own(c).start()

    fold_and_send(0)
    z_send(0)
    mine = pl.ds(pl.multiple_of(ed * PAD, PAD), SLOTS)
    pltpu.make_async_copy(hid_hbm, h4.at[mine], in_sem.at[3]).wait()
    for h in range(1, NX):
        remote(h4.at[mine], h4.at[mine], hs_sem, hr_sem, {"edata": at_x(h)}).start()

    def fold_loop(c, carry):
        select(c + 1)
        plane_send(c + 1)
        fold_and_send(c)
        z_send(c)
        return carry

    lax.fori_loop(1, SPLIT, fold_loop, 0)
    for c in range(SPLIT + 1, NCH):
        select(c)
        plane_send(c)
    fold_and_send(SPLIT)
    z_send(SPLIT, 0, 128, NCH)
    z_send(SPLIT, 128, 128 * (FOLD - 1))
    for c in range(SPLIT + 1, NCH):
        fold_and_send(c)
        z_send(c)

    n = iota((SLOTS, 1), 0)
    nz = (n * 5462) >> 16
    col = iota((SLOTS, rows), 1)
    for part in range(1 + FOLD):
        slot = folded_slot(col, part)
        unf_s[:, pl.ds(part * rows, rows)] = one_hot(((col >> 4) == nz) & (n - 12 * nz == slot))

    for x in range(NX):
        h4[pl.ds(x * PAD + SLOTS, PAD - SLOTS), :] = jnp.zeros((PAD - SLOTS, H), BF)
    proj[...] = jnp.zeros_like(proj)
    count, _, rank = named(ids, weights, iota((NZ * NJ, 1), 0))
    cnt_s[...] = count
    rank_s[...] = rank

    pltpu.make_async_copy(w_hbm, w_s, in_sem.at[4]).wait()

    eye = one_hot(iota((128, 128), 0) == iota((128, 128), 1))

    def turn(group):
        cols = pl.ds(pl.multiple_of(group * 128, 128), 128)
        part = jnp.concatenate([ar[:, cols], jnp.zeros((PAD - SLOTS, 128), BF)], axis=0)
        turned = lax.dot_general(eye, part, (((1,), (1,)), ((), ())), preferred_element_type=F32)
        xs[cols, :] = turned.astype(BF)

    def unfold_last(c):
        stacked = jnp.concatenate([zr[c, :, pl.ds(128 * k, 128)] for k in range(FOLD)], axis=0)
        last = pl.ds(pl.multiple_of(c * CH + 128 * FOLD, 128), 128)
        ar[:, last] = dot(unf_s[:, pl.ds(rows, FOLD * rows)], stacked).astype(BF)

    def chunk(c):
        z_copies(c).wait_recv()
        z_own(c).wait()
        ar[:, pl.ds(pl.multiple_of(c * CH, CH), 128 * FOLD)] = dot(unf_s[:, pl.ds(0, rows)], zr[c]).astype(BF)
        unfold_last(c)
        for g in range(FOLD + 1):
            turn(c * (FOLD + 1) + g)

    def project(c):
        cols = pl.ds(pl.multiple_of(c * CH, CH), CH)
        proj[...] += dot(ar[:, cols], w_s[cols, :])

    x_mine = pl.ds(pl.multiple_of(ed * PAD, PAD), PAD)

    def x_own(b):
        ours = pl.ds(pl.multiple_of(b * BLK + ed * OWN, 32), OWN)
        return pltpu.make_async_copy(xs.at[ours], xr.at[b, :, x_mine], xl_sem.at[b])

    def block_send(b):
        for h in range(1, NX):
            xt = at_x(h)
            theirs = pl.ds(pl.multiple_of(b * BLK + xt * OWN, 32), OWN)
            remote(xs.at[theirs], xr.at[b, :, x_mine], xs_sem.at[b], xr_sem.at[b], {"edata": xt}).start()
        x_own(b).start()

    def x_copies(b):
        return remote(
            xs.at[pl.ds(0, (NX - 1) * OWN)], xr.at[b, :, pl.ds(0, (NX - 1) * PAD)],
            xs_sem.at[b], xr_sem.at[b], {"edata": ed},
        )

    def block_product(b):
        x_own(b).wait()
        x_copies(b).wait_recv()
        return dot(xr[b], h4[...])

    def y_copy(b):
        step = jnp.where(b == 0, 2, jnp.where((b == 1) == (core == 0), 1, 3))
        return remote(ys.at[b], yr.at[b], ys_sem.at[b], yr_sem.at[b], {"dp": lax.rem(dp + step, NY)})

    def h_copies():
        some = pl.ds(0, (NX - 1) * SLOTS)
        return remote(h4.at[some], h4.at[some], hs_sem, hr_sem, {"edata": ed})

    def pair(b, carry):
        chunk(2 * b)
        project(2 * b)
        chunk(2 * b + 1)
        block_send(b)
        project(2 * b + 1)

        @pl.when(b == 0)
        def _():
            h_copies().wait_recv()

        ys[b] = block_product(b).astype(BF)
        y_copy(b).start()
        return carry

    lax.fori_loop(0, NY - 2, pair, 0)
    chunk(SPLIT - 1)
    project(SPLIT - 1)
    z_copies(SPLIT, 0, 128, NCH).wait_recv()
    z_own(SPLIT).wait()
    ar[:, pl.ds(SPLIT * CH, 128)] = dot(unf_s[:, pl.ds(0, rows)], zr[SPLIT, :, pl.ds(0, 128)]).astype(BF)
    turn(SPLIT * (FOLD + 1))
    block_send(NY - 2)
    z_copies(SPLIT, 128, 128 * (FOLD - 1)).wait_recv()
    rest = zr[SPLIT, :, pl.ds(128, 128 * (FOLD - 1))]
    ar[:, pl.ds(SPLIT * CH + 128, 128 * (FOLD - 1))] = dot(unf_s[:, pl.ds(0, rows)], rest).astype(BF)
    unfold_last(SPLIT)
    for g in range(1, FOLD + 1):
        turn(SPLIT * (FOLD + 1) + g)
    project(SPLIT)
    ys[NY - 2] = block_product(NY - 2).astype(BF)
    y_copy(NY - 2).start()
    chunk(NCH - 1)
    block_send(NY - 1)
    project(NCH - 1)

    total = proj[...]
    slot_grad = jnp.sum(total * h4[mine, :].astype(F32), axis=1, keepdims=True)
    placed = jnp.where(iota((SLOTS, 128), 1) == n - 12 * nz, slot_grad, 0.0)
    gather = (iota((NZ, SLOTS), 0) == ((iota((NZ, SLOTS), 1) * 5462) >> 16)).astype(F32)
    by_plane = exact_dot(gather, placed)
    for to in range(NZ):
        r1s[to] = jnp.broadcast_to(by_plane[to : to + 1, :], (8, 128))
    for h in OFFS:
        to = at_z(h)
        remote(r1s.at[to], r1r.at[z], r_sem.at[0], r_sem.at[1], to_z(to)).start()
    r1_own = pltpu.make_async_copy(r1s.at[z], r1r.at[z], r_sem.at[2])
    r1_own.start()
    gh_s[...] = total.astype(BF)
    gh_out = pltpu.make_async_copy(gh_s, gh_hbm, out_sem.at[0])
    gh_out.start()
    r1_own.wait()
    r1_all = remote(r1s.at[pl.ds(0, NZ - 1)], r1r.at[pl.ds(0, NZ - 1)], r_sem.at[0], r_sem.at[1], to_z(z))
    r1_all.wait_recv()
    planes = jnp.concatenate([r1r[zt, pl.ds(0, 1), :] for zt in range(NZ)], axis=0)
    j_rows = pl.ds(pl.multiple_of(j * NZ, NZ), NZ)
    r2r[j_rows, :] = planes
    for h in range(1, NJ):
        remote(r2r.at[j_rows], r2r.at[j_rows], r_sem.at[3], r_sem.at[4], to_j(at_j(h))).start()

    down = block_product(NY - 1)
    for b in range(NY - 1):
        y_copy(b).wait_recv()
        down = down + yr[b].astype(F32)
    gd_s[...] = down.astype(BF)
    gd_out = pltpu.make_async_copy(gd_s, gd_hbm, out_sem.at[1])
    gd_out.start()

    some = pl.ds(0, (NJ - 1) * NZ)
    r2_all = remote(r2r.at[some], r2r.at[some], r_sem.at[3], r_sem.at[4], to_j(j))
    r2_all.wait_recv()
    experts = NZ * NJ
    e_row = iota((experts, experts), 0)
    spread = (iota((experts, experts), 1) == (e_row & 3) * NZ + (e_row >> 2)).astype(F32)
    values = exact_dot(spread, r2r[...])
    lane = iota((experts, 128), 1) - 3 * j
    grads = jnp.zeros((experts, TOK), F32)
    for r in range(CAP):
        value = jnp.sum(jnp.where(lane == r, values, 0.0), axis=1, keepdims=True)
        grads = grads + jnp.where((cnt_s[...] > 0.0) & (rank_s[...] == float(r)), value, 0.0)
    ids = ids_s[...]
    scores = jax.nn.sigmoid(logit_s[...])
    score_sum = jnp.sum(scores, axis=0, keepdims=True)
    weights = (2.5 * scores / score_sum).astype(BF).astype(F32)
    e_col = iota((experts, 1), 0)
    picked = [
        jnp.sum(jnp.where(ids[k : k + 1, :] == e_col, grads, 0.0), axis=0, keepdims=True) for k in range(TOP)
    ]
    combine_grad = jnp.concatenate(picked, axis=0) / weights
    mean = jnp.sum(combine_grad * scores, axis=0, keepdims=True) / score_sum
    lg_s[...] = scores * (1.0 - scores) * (2.5 / score_sum) * (combine_grad - mean)
    lg_out = pltpu.make_async_copy(lg_s, lg_hbm, out_sem.at[2])
    lg_out.start()

    h_copies().wait_send()

    def drain_z(c, carry):
        z_copies(c).wait_send()
        return carry

    def drain_p(c, carry):
        plane_copies(c).wait_send()
        return carry

    def drain_x(b, carry):
        x_copies(b).wait_send()
        return carry

    def drain_y(b, carry):
        y_copy(b).wait_send()
        return carry

    lax.fori_loop(0, SPLIT, drain_z, 0)
    z_copies(SPLIT, 0, 128, NCH).wait_send()
    z_copies(SPLIT, 128, 128 * (FOLD - 1)).wait_send()
    lax.fori_loop(SPLIT + 1, NCH, drain_z, 0)
    lax.fori_loop(0, NCH, drain_p, 0)
    lax.fori_loop(0, NY, drain_x, 0)
    lax.fori_loop(0, NY - 1, drain_y, 0)
    r1_all.wait_send()
    r2_all.wait_send()
    gh_out.wait()
    gd_out.wait()
    lg_out.wait()


def on_device(out_grad, route_ids, router_logits, hidden, down_weight):
    rows = NZ * ZROWS
    dma = pltpu.SemaphoreType.DMA
    vm = pltpu.VMEM
    anywhere = pl.BlockSpec(memory_space=pl.ANY)
    grad_down, grad_hidden, logit_grad = pl.pallas_call(
        kernel,
        out_shape=(
            jax.ShapeDtypeStruct((OWN, H), BF),
            jax.ShapeDtypeStruct((SLOTS, H), BF),
            jax.ShapeDtypeStruct((TOP, TOK), F32),
        ),
        in_specs=[pl.BlockSpec(memory_space=pltpu.HBM)] * 5,
        out_specs=(anywhere,) * 3,
        scratch_shapes=[
            vm((2 * TOK, D), BF), vm((TOP, TOK), jnp.int32), vm((TOP, TOK), F32), vm((D, H), BF),
            vm((SLOTS, 2 * TOK), BF), vm(((1 + FOLD) * rows, SLOTS), BF), vm((SLOTS, (1 + FOLD) * rows), BF), vm((NX * PAD, H), BF),
            vm((NCH, rows, 128 * FOLD), BF), vm((NCH, rows, 128 * FOLD), BF), vm((NCH, SLOTS, CH), BF), vm((NCH, SLOTS, CH), BF), vm((SLOTS, D), BF),
            vm((D, PAD), BF), vm((NY, OWN, NX * PAD), BF), vm((NY - 1, OWN, H), BF), vm((NY - 1, OWN, H), BF),
            vm((SLOTS, H), F32), vm((NZ * NJ, TOK), F32), vm((NZ * NJ, TOK), F32),
            vm((NZ, 8, 128), F32), vm((NZ, 8, 128), F32), vm((NJ * NZ, 128), F32),
            vm((OWN, H), BF), vm((SLOTS, H), BF), vm((TOP, TOK), F32),
            dma((5,)), dma((3,)), dma, dma, dma((NCH + 1,)), dma((NCH + 1,)), dma((NCH,)), dma((NCH,)), dma((NCH,)), dma((NCH,)),
            dma((NY,)), dma((NY,)), dma((NY,)), dma((NY - 1,)), dma((NY - 1,)), dma((6,)),
        ],
        compiler_params=pltpu.CompilerParams(
            collective_id=0, has_side_effects=True, vmem_limit_bytes=52 << 20
        ),
        cost_estimate=pl.CostEstimate(flops=4 * SLOTS * D * H, bytes_accessed=2 * D * H, transcendentals=0),
    )(
        out_grad,
        route_ids.T,
        router_logits.T,
        hidden.reshape(SLOTS, H),
        down_weight.reshape(D, H),
    )
    return grad_down.reshape(OWN, 1, H), grad_hidden.reshape(1, 1, SLOTS, H), logit_grad.T


def solution(mesh):
    in_specs = (
        P(("dp", "edata", "expert"), None),
        P(("dp", "edata", "expert"), None),
        P(("dp", "edata", "expert"), None),
        P(("dp", "edata"), "expert", None, None),
        P(None, "expert", None),
    )
    out_specs = (
        P(("dp", "edata"), "expert", None),
        P(("dp", "edata"), "expert", None, None),
        P(("dp", "edata", "expert"), None),
    )
    return jax.shard_map(
        on_device, mesh=mesh, in_specs=in_specs, out_specs=out_specs, check_vma=False
    )
```

```python
import jax
import jax.numpy as jnp
from jax import lax
from jax.experimental import pallas as pl
from jax.experimental.pallas import tpu as pltpu
from jax.sharding import PartitionSpec as P

MESH = pl.DeviceIdType.MESH
BF = jnp.bfloat16
F32 = jnp.float32
NZ = 16
NJ = 4
NX = 4
NY = 4
CAP = 3
TOK = 128
TOP = 8
D = 3584
H = 1024
SLOTS = NZ * NJ * CAP
PLANE_ROWS = NZ * CAP
ZROWS = 16
CH = 512
NCH = D // CH
FOLD = CH // 128 - 1
BLK = D // NY
OWN = BLK // NX
PAD = 256
SPLIT = (BLK * (NY - 1)) // CH
OFFS = [8, 7, 9, 6, 10, 5, 11, 4, 12, 3, 13, 2, 14, 1, 15]


def iota(shape, axis):
    return lax.broadcasted_iota(jnp.int32, shape, axis)


def dot(a, b):
    return jnp.dot(a, b, preferred_element_type=F32)


def exact_dot(a, b):
    return jnp.dot(a, b, preferred_element_type=F32, precision=lax.Precision.HIGHEST)


def third(q):
    return (q * 11) >> 5


def send_parts(row):
    j = (row * 1366) >> 16
    rest = row - PLANE_ROWS * j
    z = (rest * 43) >> 7
    return j, z, rest - 3 * z


def folded_slot(row, part):
    q = row & 15
    if part == 0:
        return jnp.where(q < 12, q, -1)
    return jnp.where(q >= 12, 4 * (part - 1) + (q - 12), -1)


def one_hot(mask):
    return mask.astype(F32).astype(BF)


def named(ids, weights, expert):
    rows = expert.shape[0]
    count = jnp.zeros((rows, TOK), F32)
    weight = jnp.zeros((rows, TOK), F32)
    for k in range(TOP):
        hit = ids[k : k + 1, :] == expert
        count = count + jnp.where(hit, 1.0, 0.0)
        weight = weight + jnp.where(hit, weights[k : k + 1, :], 0.0)
    before = (iota((TOK, TOK), 0) < iota((TOK, TOK), 1)).astype(F32).astype(BF)
    rank = dot(count.astype(BF), before)
    return count, weight, rank


def kernel(
    og_hbm, ids_hbm, logit_hbm, hid_hbm, w_hbm,
    gd_hbm, gh_hbm, lg_hbm,
    og_s, ids_s, logit_s, w_s, sel_s, fold_s, unf_s, h4, zs, zr, ps, pr, ar, xs, xr, ys, yr, proj,
    cnt_s, rank_s, r1s, r1r, r2r, gd_s, gh_s, lg_s,
    in_sem, out_sem, hs_sem, hr_sem, zs_sem, zr_sem, zl_sem, ps_sem, pr_sem, pl_sem,
    xs_sem, xr_sem, xl_sem, ys_sem, yr_sem, r_sem,
):
    dp = lax.axis_index("dp")
    ed = lax.axis_index("edata")
    ex = lax.axis_index("expert")
    z = ex // NJ
    j = ex % NJ
    core = ex % 2

    def at_z(h):
        return lax.rem(z + h, NZ)

    def at_j(h):
        return lax.rem(j + h, NJ)

    def at_x(h):
        return lax.rem(ed + h, NX)

    def to_z(zt):
        return {"expert": zt * NJ + j}

    def to_j(jt):
        return {"expert": z * NJ + jt}

    def owner(b, c):
        step = (2, 1, 3, 0)[b] if not isinstance(c, int) else ((2, 1, 3, 0), (2, 3, 1, 0))[c][b]
        if not isinstance(c, int) and b in (1, 2):
            step = jnp.where(c == 0, step, 4 - step)
        return lax.rem(dp + step, NY)

    def remote(src, dst, ssem, rsem, where):
        return pltpu.make_async_remote_copy(
            src_ref=src, dst_ref=dst, send_sem=ssem, recv_sem=rsem, device_id=where, device_id_type=MESH
        )

    barrier = pltpu.get_barrier_semaphore()
    for h in OFFS:
        pl.semaphore_signal(barrier, inc=1, device_id=to_z(at_z(h)), device_id_type=MESH)
    for h in range(1, 4):
        pl.semaphore_signal(barrier, inc=1, device_id=to_j(at_j(h)), device_id_type=MESH)
        pl.semaphore_signal(barrier, inc=1, device_id={"edata": at_x(h)}, device_id_type=MESH)
        pl.semaphore_signal(barrier, inc=1, device_id={"dp": lax.rem(dp + h, NY)}, device_id_type=MESH)

    pltpu.make_async_copy(ids_hbm, ids_s, in_sem.at[0]).start()
    pltpu.make_async_copy(logit_hbm, logit_s, in_sem.at[1]).start()
    for c in range(2):
        for b in range(NY):
            start = pl.multiple_of(owner(b, c) * BLK, BLK)
            pltpu.make_async_copy(
                og_hbm.at[:, pl.ds(start, BLK)],
                og_s.at[pl.ds(c * TOK, TOK), pl.ds(b * BLK, BLK)],
                in_sem.at[2],
            ).start()
    pltpu.make_async_copy(hid_hbm, h4.at[pl.ds(pl.multiple_of(ed * PAD, PAD), SLOTS)], in_sem.at[3]).start()
    for b in range(NY):
        start = pl.multiple_of(owner(b, core) * BLK, BLK)
        pltpu.make_async_copy(
            w_hbm.at[pl.ds(start, BLK)], w_s.at[pl.ds(b * BLK, BLK)], in_sem.at[4]
        ).start()

    pltpu.make_async_copy(ids_hbm, ids_s, in_sem.at[0]).wait()
    pltpu.make_async_copy(logit_hbm, logit_s, in_sem.at[1]).wait()
    ids = ids_s[...]
    scores = jax.nn.sigmoid(logit_s[...])
    score_sum = jnp.sum(scores, axis=0, keepdims=True)
    weights = (2.5 * scores / score_sum).astype(BF).astype(F32)
    rows = NZ * ZROWS
    jt, zt, rank_of = send_parts(iota((SLOTS, 1), 0))
    count, weight, rank = named(ids, weights, zt * NJ + jt)
    chosen = jnp.where((count > 0.0) & (rank == rank_of.astype(F32)), weight, 0.0)
    odd = (jt & 1) == 1
    sel_s[:, pl.ds(0, TOK)] = jnp.where(odd, 0.0, chosen).astype(BF)
    sel_s[:, pl.ds(TOK, TOK)] = jnp.where(odd, chosen, 0.0).astype(BF)
    pltpu.make_async_copy(og_s, og_s, in_sem.at[2]).wait()

    z_mine = pl.ds(pl.multiple_of(z * ZROWS, ZROWS), ZROWS)
    j_mine = pl.ds(pl.multiple_of(j * PLANE_ROWS, PLANE_ROWS), PLANE_ROWS)

    def select(c):
        cols = pl.ds(pl.multiple_of(c * CH, CH), CH)
        ps[c] = dot(sel_s[...], og_s[:, cols]).astype(BF)

    def plane_send(c):
        for h in range(1, NJ):
            to = at_j(h)
            theirs = pl.ds(pl.multiple_of(to * PLANE_ROWS, PLANE_ROWS), PLANE_ROWS)
            remote(ps.at[c, theirs], pr.at[c, j_mine], ps_sem.at[c], pr_sem.at[c], to_j(to)).start()
        pltpu.make_async_copy(ps.at[c, j_mine], pr.at[c, j_mine], pl_sem.at[c]).start()

    def plane_copies(c):
        some = pl.ds(0, (NJ - 1) * PLANE_ROWS)
        return remote(ps.at[c, some], pr.at[c, some], ps_sem.at[c], pr_sem.at[c], to_j(j))

    def fold(c):
        plain = dot(fold_s[pl.ds(0, rows), :], pr[c, :, pl.ds(0, 128 * FOLD)])
        last = dot(fold_s[pl.ds(rows, FOLD * rows), :], pr[c, :, pl.ds(128 * FOLD, 128)])
        for k in range(FOLD):
            part = plain[:, 128 * k : 128 * (k + 1)] + last[rows * k : rows * (k + 1)]
            zs[c, :, pl.ds(128 * k, 128)] = part.astype(BF)

    def z_send(c, first=0, width=128 * FOLD, at=None):
        at = c if at is None else at
        part = pl.ds(first, width)
        for h in OFFS:
            to = at_z(h)
            theirs = pl.ds(pl.multiple_of(to * ZROWS, ZROWS), ZROWS)
            remote(
                zs.at[c, theirs, part], zr.at[c, z_mine, part], zs_sem.at[at], zr_sem.at[at], to_z(to)
            ).start()

    def z_own(c):
        return pltpu.make_async_copy(zs.at[c, z_mine], zr.at[c, z_mine], zl_sem.at[c])

    def z_copies(c, first=0, width=128 * FOLD, at=None):
        at = c if at is None else at
        some, part = pl.ds(0, (NZ - 1) * ZROWS), pl.ds(first, width)
        return remote(zs.at[c, some, part], zr.at[c, some, part], zs_sem.at[at], zr_sem.at[at], to_z(z))

    select(0)
    pl.semaphore_wait(barrier, NZ - 1 + 9)
    plane_send(0)
    select(1)
    plane_send(1)

    row = iota((rows, 1), 0)
    cj, cz, crank = send_parts(iota((rows, SLOTS), 1))
    for part in range(1 + FOLD):
        slot = folded_slot(row, part)
        fold_s[pl.ds(part * rows, rows), :] = one_hot((cz == (row >> 4)) & (3 * cj + crank == slot))
    def fold_and_send(c):
        pltpu.make_async_copy(ps.at[c, j_mine], pr.at[c, j_mine], pl_sem.at[c]).wait()
        plane_copies(c).wait_recv()
        fold(c)
        z_own(c).start()

    fold_and_send(0)
    z_send(0)
    mine = pl.ds(pl.multiple_of(ed * PAD, PAD), SLOTS)
    pltpu.make_async_copy(hid_hbm, h4.at[mine], in_sem.at[3]).wait()
    for h in range(1, NX):
        remote(h4.at[mine], h4.at[mine], hs_sem, hr_sem, {"edata": at_x(h)}).start()

    def fold_loop(c, carry):
        select(c + 1)
        plane_send(c + 1)
        fold_and_send(c)
        z_send(c)
        return carry

    lax.fori_loop(1, SPLIT, fold_loop, 0)
    for c in range(SPLIT + 1, NCH):
        select(c)
        plane_send(c)
    fold_and_send(SPLIT)
    z_send(SPLIT, 0, 128, NCH)
    z_send(SPLIT, 128, 128 * (FOLD - 1))
    for c in range(SPLIT + 1, NCH):
        fold_and_send(c)
        z_send(c)

    n = iota((SLOTS, 1), 0)
    nz = (n * 5462) >> 16
    col = iota((SLOTS, rows), 1)
    for part in range(1 + FOLD):
        slot = folded_slot(col, part)
        unf_s[:, pl.ds(part * rows, rows)] = one_hot(((col >> 4) == nz) & (n - 12 * nz == slot))

    for x in range(NX):
        h4[pl.ds(x * PAD + SLOTS, PAD - SLOTS), :] = jnp.zeros((PAD - SLOTS, H), BF)
    proj[...] = jnp.zeros_like(proj)
    count, _, rank = named(ids, weights, iota((NZ * NJ, 1), 0))
    cnt_s[...] = count
    rank_s[...] = rank

    pltpu.make_async_copy(w_hbm, w_s, in_sem.at[4]).wait()

    eye = one_hot(iota((128, 128), 0) == iota((128, 128), 1))

    def turn(group):
        cols = pl.ds(pl.multiple_of(group * 128, 128), 128)
        part = jnp.concatenate([ar[:, cols], jnp.zeros((PAD - SLOTS, 128), BF)], axis=0)
        turned = lax.dot_general(eye, part, (((1,), (1,)), ((), ())), preferred_element_type=F32)
        xs[cols, :] = turned.astype(BF)

    def unfold_last(c):
        stacked = jnp.concatenate([zr[c, :, pl.ds(128 * k, 128)] for k in range(FOLD)], axis=0)
        last = pl.ds(pl.multiple_of(c * CH + 128 * FOLD, 128), 128)
        ar[:, last] = dot(unf_s[:, pl.ds(rows, FOLD * rows)], stacked).astype(BF)

    def chunk(c):
        z_copies(c).wait_recv()
        z_own(c).wait()
        ar[:, pl.ds(pl.multiple_of(c * CH, CH), 128 * FOLD)] = dot(unf_s[:, pl.ds(0, rows)], zr[c]).astype(BF)
        unfold_last(c)
        for g in range(FOLD + 1):
            turn(c * (FOLD + 1) + g)

    def project(c):
        cols = pl.ds(pl.multiple_of(c * CH, CH), CH)
        proj[...] += dot(ar[:, cols], w_s[cols, :])

    x_mine = pl.ds(pl.multiple_of(ed * PAD, PAD), PAD)

    def x_own(b):
        ours = pl.ds(pl.multiple_of(b * BLK + ed * OWN, 32), OWN)
        return pltpu.make_async_copy(xs.at[ours], xr.at[b, :, x_mine], xl_sem.at[b])

    def block_send(b):
        for h in range(1, NX):
            xt = at_x(h)
            theirs = pl.ds(pl.multiple_of(b * BLK + xt * OWN, 32), OWN)
            remote(xs.at[theirs], xr.at[b, :, x_mine], xs_sem.at[b], xr_sem.at[b], {"edata": xt}).start()
        x_own(b).start()

    def x_copies(b):
        return remote(
            xs.at[pl.ds(0, (NX - 1) * OWN)], xr.at[b, :, pl.ds(0, (NX - 1) * PAD)],
            xs_sem.at[b], xr_sem.at[b], {"edata": ed},
        )

    def block_product(b):
        x_own(b).wait()
        x_copies(b).wait_recv()
        return dot(xr[b], h4[...])

    def y_copy(b):
        step = jnp.where(b == 0, 2, jnp.where((b == 1) == (core == 0), 1, 3))
        return remote(ys.at[b], yr.at[b], ys_sem.at[b], yr_sem.at[b], {"dp": lax.rem(dp + step, NY)})

    def h_copies():
        some = pl.ds(0, (NX - 1) * SLOTS)
        return remote(h4.at[some], h4.at[some], hs_sem, hr_sem, {"edata": ed})

    def pair(b, carry):
        chunk(2 * b)
        project(2 * b)
        chunk(2 * b + 1)
        block_send(b)
        project(2 * b + 1)

        @pl.when(b == 0)
        def _():
            h_copies().wait_recv()

        ys[b] = block_product(b).astype(BF)
        y_copy(b).start()
        return carry

    lax.fori_loop(0, NY - 2, pair, 0)
    chunk(SPLIT - 1)
    project(SPLIT - 1)
    z_copies(SPLIT, 0, 128, NCH).wait_recv()
    z_own(SPLIT).wait()
    ar[:, pl.ds(SPLIT * CH, 128)] = dot(unf_s[:, pl.ds(0, rows)], zr[SPLIT, :, pl.ds(0, 128)]).astype(BF)
    turn(SPLIT * (FOLD + 1))
    block_send(NY - 2)
    z_copies(SPLIT, 128, 128 * (FOLD - 1)).wait_recv()
    rest = zr[SPLIT, :, pl.ds(128, 128 * (FOLD - 1))]
    ar[:, pl.ds(SPLIT * CH + 128, 128 * (FOLD - 1))] = dot(unf_s[:, pl.ds(0, rows)], rest).astype(BF)
    unfold_last(SPLIT)
    for g in range(1, FOLD + 1):
        turn(SPLIT * (FOLD + 1) + g)
    project(SPLIT)
    ys[NY - 2] = block_product(NY - 2).astype(BF)
    y_copy(NY - 2).start()
    chunk(NCH - 1)
    block_send(NY - 1)
    project(NCH - 1)

    total = proj[...]
    slot_grad = jnp.sum(total * h4[mine, :].astype(F32), axis=1, keepdims=True)
    placed = jnp.where(iota((SLOTS, 128), 1) == n - 12 * nz, slot_grad, 0.0)
    gather = (iota((NZ, SLOTS), 0) == ((iota((NZ, SLOTS), 1) * 5462) >> 16)).astype(F32)
    by_plane = exact_dot(gather, placed)
    for to in range(NZ):
        r1s[to] = jnp.broadcast_to(by_plane[to : to + 1, :], (8, 128))
    for h in OFFS:
        to = at_z(h)
        remote(r1s.at[to], r1r.at[z], r_sem.at[0], r_sem.at[1], to_z(to)).start()
    r1_own = pltpu.make_async_copy(r1s.at[z], r1r.at[z], r_sem.at[2])
    r1_own.start()
    gh_s[...] = total.astype(BF)
    gh_out = pltpu.make_async_copy(gh_s, gh_hbm, out_sem.at[0])
    gh_out.start()
    r1_own.wait()
    r1_all = remote(r1s.at[pl.ds(0, NZ - 1)], r1r.at[pl.ds(0, NZ - 1)], r_sem.at[0], r_sem.at[1], to_z(z))
    r1_all.wait_recv()
    planes = jnp.concatenate([r1r[zt, pl.ds(0, 1), :] for zt in range(NZ)], axis=0)
    j_rows = pl.ds(pl.multiple_of(j * NZ, NZ), NZ)
    r2r[j_rows, :] = planes
    for h in range(1, NJ):
        remote(r2r.at[j_rows], r2r.at[j_rows], r_sem.at[3], r_sem.at[4], to_j(at_j(h))).start()

    down = block_product(NY - 1)
    for b in range(NY - 1):
        y_copy(b).wait_recv()
        down = down + yr[b].astype(F32)
    gd_s[...] = down.astype(BF)
    gd_out = pltpu.make_async_copy(gd_s, gd_hbm, out_sem.at[1])
    gd_out.start()

    h_copies().wait_send()

    def drain_z(c, carry):
        z_copies(c).wait_send()
        return carry

    def drain_p(c, carry):
        plane_copies(c).wait_send()
        return carry

    def drain_x(b, carry):
        x_copies(b).wait_send()
        return carry

    def drain_y(b, carry):
        y_copy(b).wait_send()
        return carry

    lax.fori_loop(0, SPLIT, drain_z, 0)
    z_copies(SPLIT, 0, 128, NCH).wait_send()
    z_copies(SPLIT, 128, 128 * (FOLD - 1)).wait_send()
    lax.fori_loop(SPLIT + 1, NCH, drain_z, 0)
    lax.fori_loop(0, NCH, drain_p, 0)
    lax.fori_loop(0, NY, drain_x, 0)
    lax.fori_loop(0, NY - 1, drain_y, 0)
    r1_all.wait_send()

    some = pl.ds(0, (NJ - 1) * NZ)
    r2_all = remote(r2r.at[some], r2r.at[some], r_sem.at[3], r_sem.at[4], to_j(j))
    r2_all.wait_recv()
    experts = NZ * NJ
    e_row = iota((experts, experts), 0)
    spread = (iota((experts, experts), 1) == (e_row & 3) * NZ + (e_row >> 2)).astype(F32)
    values = exact_dot(spread, r2r[...])
    lane = iota((experts, 128), 1) - 3 * j
    grads = jnp.zeros((experts, TOK), F32)
    for r in range(CAP):
        value = jnp.sum(jnp.where(lane == r, values, 0.0), axis=1, keepdims=True)
        grads = grads + jnp.where((cnt_s[...] > 0.0) & (rank_s[...] == float(r)), value, 0.0)
    ids = ids_s[...]
    scores = jax.nn.sigmoid(logit_s[...])
    score_sum = jnp.sum(scores, axis=0, keepdims=True)
    weights = (2.5 * scores / score_sum).astype(BF).astype(F32)
    e_col = iota((experts, 1), 0)
    picked = [
        jnp.sum(jnp.where(ids[k : k + 1, :] == e_col, grads, 0.0), axis=0, keepdims=True) for k in range(TOP)
    ]
    combine_grad = jnp.concatenate(picked, axis=0) / weights
    mean = jnp.sum(combine_grad * scores, axis=0, keepdims=True) / score_sum
    lg_s[...] = scores * (1.0 - scores) * (2.5 / score_sum) * (combine_grad - mean)
    lg_out = pltpu.make_async_copy(lg_s, lg_hbm, out_sem.at[2])
    lg_out.start()
    r2_all.wait_send()
    gh_out.wait()
    gd_out.wait()
    lg_out.wait()


def on_device(out_grad, route_ids, router_logits, hidden, down_weight):
    rows = NZ * ZROWS
    dma = pltpu.SemaphoreType.DMA
    vm = pltpu.VMEM
    anywhere = pl.BlockSpec(memory_space=pl.ANY)
    grad_down, grad_hidden, logit_grad = pl.pallas_call(
        kernel,
        out_shape=(
            jax.ShapeDtypeStruct((OWN, H), BF),
            jax.ShapeDtypeStruct((SLOTS, H), BF),
            jax.ShapeDtypeStruct((TOP, TOK), F32),
        ),
        in_specs=[pl.BlockSpec(memory_space=pltpu.HBM)] * 5,
        out_specs=(anywhere,) * 3,
        scratch_shapes=[
            vm((2 * TOK, D), BF), vm((TOP, TOK), jnp.int32), vm((TOP, TOK), F32), vm((D, H), BF),
            vm((SLOTS, 2 * TOK), BF), vm(((1 + FOLD) * rows, SLOTS), BF), vm((SLOTS, (1 + FOLD) * rows), BF), vm((NX * PAD, H), BF),
            vm((NCH, rows, 128 * FOLD), BF), vm((NCH, rows, 128 * FOLD), BF), vm((NCH, SLOTS, CH), BF), vm((NCH, SLOTS, CH), BF), vm((SLOTS, D), BF),
            vm((D, PAD), BF), vm((NY, OWN, NX * PAD), BF), vm((NY - 1, OWN, H), BF), vm((NY - 1, OWN, H), BF),
            vm((SLOTS, H), F32), vm((NZ * NJ, TOK), F32), vm((NZ * NJ, TOK), F32),
            vm((NZ, 8, 128), F32), vm((NZ, 8, 128), F32), vm((NJ * NZ, 128), F32),
            vm((OWN, H), BF), vm((SLOTS, H), BF), vm((TOP, TOK), F32),
            dma((5,)), dma((3,)), dma, dma, dma((NCH + 1,)), dma((NCH + 1,)), dma((NCH,)), dma((NCH,)), dma((NCH,)), dma((NCH,)),
            dma((NY,)), dma((NY,)), dma((NY,)), dma((NY - 1,)), dma((NY - 1,)), dma((6,)),
        ],
        compiler_params=pltpu.CompilerParams(
            collective_id=0, has_side_effects=True, vmem_limit_bytes=52 << 20
        ),
        cost_estimate=pl.CostEstimate(flops=4 * SLOTS * D * H, bytes_accessed=2 * D * H, transcendentals=0),
    )(
        out_grad,
        route_ids.T,
        router_logits.T,
        hidden.reshape(SLOTS, H),
        down_weight.reshape(D, H),
    )
    return grad_down.reshape(OWN, 1, H), grad_hidden.reshape(1, 1, SLOTS, H), logit_grad.T


def solution(mesh):
    in_specs = (
        P(("dp", "edata", "expert"), None),
        P(("dp", "edata", "expert"), None),
        P(("dp", "edata", "expert"), None),
        P(("dp", "edata"), "expert", None, None),
        P(None, "expert", None),
    )
    out_specs = (
        P(("dp", "edata"), "expert", None),
        P(("dp", "edata"), "expert", None, None),
        P(("dp", "edata", "expert"), None),
    )
    return jax.shard_map(
        on_device, mesh=mesh, in_specs=in_specs, out_specs=out_specs, check_vma=False
    )
```
